32 devices in a mesh: blk: 8 (over z, y), group: 4 (over x, core).
Axes of the slice: x: 2, y: 2, z: 4, core: 2. Of those that a mesh axis runs over, the one named last changes fastest.
Arguments:
- frames: bfloat16 [4, 1024, 1024], P('group', 'blk'), may hold values from -6 to 6
- skip_in: bfloat16 [4, 1024, 1024], P('group', 'blk'), may hold values from -6 to 6
- lengths: int32 [4, 8], P('group'), may hold values from 1 to 957, as said below
- voiced: int32 [4, 8], P('group'), may hold values from 1 to 957, as said below
- time_steps: int32 [4, 8], P('group'), may hold values from 0 to 31
- time_table: bfloat16 [32, 1024], replicated, may hold values from -6 to 6
- skip_weight: bfloat16 [2048, 1024], replicated, may hold values from -0.125 to 0.125
- skip_bias: bfloat16 [1024], replicated, may hold values from -2 to 2
- adaptive_weight: bfloat16 [1024, 4096], replicated, may hold values from -0.1875 to 0.1875
- adaptive_bias: bfloat16 [4096], replicated, may hold values from -2 to 2
- merged_weight: bfloat16 [1024, 3072], replicated, may hold values from -0.1875 to 0.1875
- output_weight: bfloat16 [1024, 1024], replicated, may hold values from -2 to 2
- output_bias: bfloat16 [1024], replicated, may hold values from -2 to 2
- up_weight: bfloat16 [1024, 4096], replicated, may hold values from -0.1875 to 0.1875
- up_bias: bfloat16 [4096], replicated, may hold values from -2 to 2
- down_weight: bfloat16 [4096, 1024], replicated, may hold values from -0.09375 to 0.09375
- down_bias: bfloat16 [1024], replicated, may hold values from -2 to 2
- cotangent: bfloat16 [4, 1024, 1024], P('group', 'blk'), may hold values from -6 to 6
Outputs:
- layer_out: bfloat16 [4, 1024, 1024], P('group', 'blk')
- frames_grad: bfloat16 [4, 1024, 1024], P('group', 'blk')
- skip_grad: bfloat16 [4, 1024, 1024], P('group', 'blk')
- table_grad: float32 [32, 1024], P(None, 'blk')
- skip_weight_grad: float32 [2048, 1024], P('blk')
- skip_bias_grad: float32 [1024], P('blk')
- adaptive_weight_grad: float32 [1024, 4096], P('blk')
- adaptive_bias_grad: float32 [4096], P('blk')
- merged_weight_grad: float32 [1024, 3072], P('blk')
- output_weight_grad: float32 [1024, 1024], P('blk')
- output_bias_grad: float32 [1024], P('blk')
- up_weight_grad: float32 [1024, 4096], P('blk')
- up_bias_grad: float32 [4096], P('blk')
- down_weight_grad: float32 [4096, 1024], P('blk')
- down_bias_grad: float32 [1024], P('blk')
The draws below stay inside these ranges and needn't reach their ends.
Inputs may be any that keep to these rules, and one draw needn't show every extreme that they name: In each group the lengths sum to 1024. One slot, at a place drawn from the seed, holds exactly the largest length; every other slot holds at most 16 frames. Each is at most the length of its slot and at least three quarters of it; the rest of the slot is padding that no query may attend to. The longest slot of a group is fully voiced.
All inputs are finite; a program needn't handle non-finite values.
Results may differ from the reference program's by a relative error of at most 0.022.
Values may be sent and summed in bfloat16 or wider, within the bound.
A program may use at most 256 MiB of HBM per device.

```python
from functools import partial
import jax
import jax.numpy as jnp
from jax import lax

D = 1024
HEADS = 16
HD = 64
FF = 4096
TOK_DEV = 128
UTT = 8
STEPS = 32
SEQ = 1024
GROUPS = 4


def utterance_plan(key):
    length_key, place_key, cut_key = jax.random.split(key, 3)
    short_most = TOK_DEV // UTT
    count = UTT - 1
    pairs = count // 2
    picks = jax.random.randint(length_key, (UTT,), 1, short_most + 1).astype(jnp.int32)
    picks = picks.at[0].set(1)
    slot = jnp.arange(count, dtype=jnp.int32)
    mirror = count - 1 - slot
    front_part = jnp.take(picks, jnp.minimum(slot, UTT - 1))
    back_part = (short_most + 1 - jnp.take(picks, jnp.minimum(mirror, UTT - 1))).astype(jnp.int32)
    short = jnp.where(slot < pairs, front_part, jnp.where(mirror < pairs, back_part, short_most)).astype(jnp.int32)
    place = jax.random.randint(place_key, (), 0, UTT)
    index = jnp.arange(UTT, dtype=jnp.int32)
    chosen = index == place
    source = jnp.clip(jnp.where(index > place, index - 1, index), 0, count - 1)
    spread = jnp.take(short, source)
    rest = jnp.sum(short).astype(jnp.int32)
    lengths = jnp.where(chosen, SEQ - rest, spread).astype(jnp.int32)
    cut = jax.random.randint(cut_key, (UTT,), 0, lengths // 4 + 1).astype(jnp.int32)
    cut = jnp.where(chosen, 0, cut).astype(jnp.int32)
    return (lengths, (lengths - cut).astype(jnp.int32))


def utterance_table(key):
    return jax.vmap(utterance_plan)(jax.random.split(key, GROUPS))


def draw_lengths(key, part):
    return utterance_table(key)[0]


def draw_voiced(key, part):
    return utterance_table(key)[1]


def plant(values, own_key, smallest, largest):
    shape = values.shape
    spot = [jax.random.randint(jax.random.fold_in(own_key, axis), (), 0, shape[axis]) for axis in range(len(shape))]
    values = values.at[tuple(spot)].set(smallest)
    longest = shape.index(max(shape))
    spot[longest] = (spot[longest] + 1) % shape[longest]
    return values.at[tuple(spot)].set(largest)


def shard_levels(stream_key, dims, shards, smallest, high):
    gain, own = 1.0, jax.random.fold_in(stream_key, 6)
    for dim, parts in shards:
        draws = jnp.exp(jax.random.uniform(jax.random.fold_in(own, dim), (parts,), jnp.float32, smallest / len(shards), high / len(shards)))
        gain = gain * jnp.repeat(draws, dims[dim] // parts).reshape([-1 if axis == dim else 1 for axis in range(len(dims))])
    return gain


def normal_values(own_key, dims, scale, reach, cuts=(), held_as=jnp.bfloat16):
    factor_of = shard_levels(own_key, dims, cuts, -0.22, 0.18) if cuts else 1.0
    array = jax.random.normal(own_key, dims, jnp.float32) * scale * factor_of
    return jnp.minimum(jnp.maximum(array, -reach), reach).astype(held_as)


def setup_inputs(seed: int = 0) -> dict:
    splits = jax.random.split(jax.random.key(seed), 19)
    frames = normal_values(splits[0], (GROUPS, SEQ, D), 1.0, 6.0, ((0, 4), (1, 8)))
    skip_in = normal_values(splits[1], (GROUPS, SEQ, D), 1.0, 6.0, ((0, 4), (1, 8)))
    lengths = draw_lengths(jax.random.fold_in(splits[18], 71), 0)
    voiced = draw_voiced(jax.random.fold_in(splits[18], 71), 0)
    time_steps = plant(jax.random.randint(splits[4], (GROUPS, UTT), 0, STEPS), jax.random.fold_in(splits[4], 1), 0, STEPS - 1).astype(jnp.int32)
    time_table = normal_values(splits[5], (STEPS, D), 1.0, 6.0)
    skip_weight = normal_values(splits[6], (2 * D, D), (2 * D) ** -0.5, 0.125)
    skip_bias = normal_values(splits[7], (D,), 0.3, 2.0)
    adaptive_weight = normal_values(splits[8], (D, 4 * D), D ** -0.5, 0.1875)
    adaptive_bias = normal_values(splits[9], (4 * D,), 0.3, 2.0)
    merged_weight = normal_values(splits[10], (D, 3 * D), D ** -0.5, 0.1875)
    output_weight = normal_values(splits[11], (D, D), (max(1, 8 * D // SEQ)) ** -0.5, 2.0)
    output_bias = normal_values(splits[12], (D,), 0.3, 2.0)
    up_weight = normal_values(splits[13], (D, FF), D ** -0.5, 0.1875)
    up_bias = normal_values(splits[14], (FF,), 0.3, 2.0)
    down_weight = normal_values(splits[15], (FF, D), FF ** -0.5, 0.09375)
    down_bias = normal_values(splits[16], (D,), 0.3, 2.0)
    cotangent = normal_values(splits[17], (GROUPS, SEQ, D), 1.0, 6.0, ((0, 4), (1, 8)))
    return {"frames": frames, "skip_in": skip_in, "lengths": lengths, "voiced": voiced, "time_steps": time_steps, "time_table": time_table, "skip_weight": skip_weight, "skip_bias": skip_bias, "adaptive_weight": adaptive_weight, "adaptive_bias": adaptive_bias, "merged_weight": merged_weight, "output_weight": output_weight, "output_bias": output_bias, "up_weight": up_weight, "up_bias": up_bias, "down_weight": down_weight, "down_bias": down_bias, "cotangent": cotangent}


EPSILON = 1e-06
SCALE = 0.125
HIGHEST = lax.Precision.HIGHEST

@jax.custom_vjp
def low(v):
    return lax.optimization_barrier(v.astype(jnp.bfloat16)).astype(jnp.float32)

@jax.custom_vjp
def low_back(v):
    return v

def low_keep(v):
    return (low(v), None)

def low_pass(kept, grad):
    return (grad,)

def back_keep(v):
    return (v, None)

def back_low(kept, grad):
    return (low(grad),)
low.defvjp(low_keep, low_pass)
low_back.defvjp(back_keep, back_low)

def hdot(left, right):
    return jnp.dot(left, right, precision=HIGHEST)

def frame_facts(lengths, voiced, position):
    ends = jnp.cumsum(lengths).astype(jnp.int32)
    begins = ends - lengths
    segment = lax.optimization_barrier(jnp.sum((position[:, None] >= ends[None, :]).astype(jnp.int32), axis=1))
    member = segment[:, None] == jnp.arange(lengths.shape[0], dtype=jnp.int32)[None, :]
    offset = position - lax.optimization_barrier(jnp.sum(jnp.where(member, begins[None, :], 0), axis=1))
    limit = lax.optimization_barrier(jnp.sum(jnp.where(member, voiced[None, :], 0), axis=1))
    return (segment, offset, offset < limit, member.astype(jnp.float32))

def turn_tables(offset, head_size):
    half = head_size // 2
    freq = 10000.0 ** (-jnp.arange(half, dtype=jnp.float32) * 2.0 / head_size)
    angle = offset.astype(jnp.float32)[:, None] * freq[None, :]
    return (jnp.cos(angle), jnp.sin(angle))

def rotate(values, cosine, sine):
    half = values.shape[-1] // 2
    front = values[..., :half]
    behind = values[..., half:]
    cos_part = cosine[:, None, :]
    sin_part = sine[:, None, :]
    return jnp.concatenate([front * cos_part - behind * sin_part, behind * cos_part + front * sin_part], axis=-1)

def adaptive_norm(hidden, scale, shift):
    mean = lax.optimization_barrier(jnp.mean(hidden, axis=-1, keepdims=True))
    centred = hidden - mean
    variance = lax.optimization_barrier(jnp.mean(centred * centred, axis=-1, keepdims=True))
    return centred * lax.rsqrt(variance + EPSILON) * (1.0 + scale) + shift

def attend_block(keys, values, segment, valid, pair):
    query_rows, query_segment = pair
    scores = low_back(jnp.einsum('qhd,khd->hqk', query_rows, keys, precision=HIGHEST)) * SCALE
    allow = (query_segment[:, None] == segment[None, :]) & valid[None, :]
    expo = jnp.where(allow[None, :, :], jnp.exp(scores), 0.0)
    total = lax.optimization_barrier(jnp.sum(expo, axis=2))
    numer = low_back(jnp.einsum('hqk,khd->qhd', low(expo), values, precision=HIGHEST))
    return numer / jnp.transpose(total)[:, :, None]

def attend(query, keys, values, segment, valid):
    count = query.shape[0]
    block = math_gcd(count, 512)
    pieces = (query.reshape(count // block, block, HEADS, HD), segment.reshape(count // block, block))
    mixed = lax.map(jax.checkpoint(partial(attend_block, keys, values, segment, valid)), pieces)
    return mixed.reshape(count, HEADS, HD)

def math_gcd(first, second):
    while second:
        first, second = (second, first % second)
    return first

def layer(frames_in, skip_part, weights, member, step_hot, cosine, sine, segment, valid):
    table, skip_weight, skip_bias, adaptive_weight, adaptive_bias, merged_weight, output_weight, output_bias, up_weight, up_bias, down_weight, down_bias = weights
    width = frames_in.shape[1]
    count = frames_in.shape[0]
    embed = hdot(step_hot, table)
    cond = low(jax.nn.silu(embed))
    modulate = hdot(member, hdot(cond, adaptive_weight) + adaptive_bias)
    first = low_back(hdot(jnp.concatenate([frames_in, skip_part], axis=1), skip_weight) + skip_bias)
    normed = low(adaptive_norm(first, modulate[:, :width], modulate[:, width:2 * width]))
    merged = low_back(hdot(normed, merged_weight))
    query = low(rotate(merged[:, :width].reshape(count, HEADS, HD), cosine, sine))
    keys = low(rotate(merged[:, width:2 * width].reshape(count, HEADS, HD), cosine, sine))
    values = low(merged[:, 2 * width:].reshape(count, HEADS, HD))
    mixed = attend(query, keys, values, segment, valid).reshape(count, width)
    attended = low_back(hdot(low(mixed), output_weight) + output_bias)
    second = first + attended
    normed_two = low(adaptive_norm(second, modulate[:, 2 * width:3 * width], modulate[:, 3 * width:]))
    hidden = low_back(hdot(normed_two, up_weight) + up_bias)
    activated = low(jax.nn.gelu(hidden))
    return second + hdot(activated, down_weight) + down_bias

def reference(frames, skip_in, lengths, voiced, time_steps, time_table, skip_weight, skip_bias, adaptive_weight, adaptive_bias, merged_weight, output_weight, output_bias, up_weight, up_bias, down_weight, down_bias, cotangent):
    params = tuple((value.astype(jnp.float32) for value in (time_table, skip_weight, skip_bias, adaptive_weight, adaptive_bias, merged_weight, output_weight, output_bias, up_weight, up_bias, down_weight, down_bias)))
    outputs = []
    frame_grads = []
    skip_grads = []
    sums = None
    for group in range(GROUPS):
        position = jnp.arange(SEQ, dtype=jnp.int32)
        segment, offset, valid, member = frame_facts(lengths[group], voiced[group], position)
        step_hot = (time_steps[group][:, None] == jnp.arange(STEPS, dtype=jnp.int32)[None, :]).astype(jnp.float32)
        cosine, sine = turn_tables(offset, HD)

        def forward(frames_in, skip_part, *weights):
            return layer(frames_in, skip_part, weights, member, step_hot, cosine, sine, segment, valid)
        result, back = jax.vjp(forward, frames[group].astype(jnp.float32), skip_in[group].astype(jnp.float32), *params)
        grads = back(cotangent[group].astype(jnp.float32))
        outputs.append(result.astype(jnp.bfloat16))
        frame_grads.append(grads[0].astype(jnp.bfloat16))
        skip_grads.append(grads[1].astype(jnp.bfloat16))
        if sums is None:
            sums = tuple(grads[2:])
        else:
            sums = tuple((held + added for held, added in zip(sums, grads[2:])))
    return (jnp.stack(outputs), jnp.stack(frame_grads), jnp.stack(skip_grads), sums[0], sums[1], sums[2], sums[3], sums[4], sums[5], sums[6], sums[7], sums[8], sums[9], sums[10], sums[11])
```

```python
import functools
import math

import jax
import jax.numpy as jnp
from jax import lax
from jax.experimental import pallas as pl
from jax.experimental.pallas import tpu as pltpu
from jax.sharding import PartitionSpec as P

HEADS = 16
HD = 64
LANES = 128
MESH_ID = pl.DeviceIdType.MESH
VMEM_SPEC = pl.BlockSpec(memory_space=pltpu.VMEM)
VMEM_LIMIT = 58 * 2**20


EPSILON = 1e-06
SCALE = 0.125
HIGHEST = lax.Precision.HIGHEST


def frame_facts(lengths, voiced, position):
    ends = jnp.cumsum(lengths)
    begins = ends - lengths
    segment = jnp.sum((position[:, None] >= ends[None, :]).astype(jnp.int32), axis=1)
    member = segment[:, None] == jnp.arange(lengths.shape[0], dtype=jnp.int32)[None, :]
    offset = position - jnp.sum(jnp.where(member, begins[None, :], 0), axis=1)
    limit = jnp.sum(jnp.where(member, voiced[None, :], 0), axis=1)
    return (segment, offset, offset < limit, member.astype(jnp.float32))


def turn_tables(offset, head_size):
    half = head_size // 2
    freq = 10000.0 ** (-jnp.arange(half, dtype=jnp.float32) * 2.0 / head_size)
    angle = offset.astype(jnp.float32)[:, None] * freq[None, :]
    return (jnp.cos(angle), jnp.sin(angle))


def rotate(values, cosine, sine):
    half = values.shape[-1] // 2
    front = values[..., :half]
    behind = values[..., half:]
    cos_part = cosine[:, None, :]
    sin_part = sine[:, None, :]
    return jnp.concatenate(
        [front * cos_part - behind * sin_part, behind * cos_part + front * sin_part], axis=-1
    )


def adaptive_norm(hidden, scale, shift):
    mean = jnp.mean(hidden, axis=-1, keepdims=True)
    centred = hidden - mean
    variance = jnp.mean(centred * centred, axis=-1, keepdims=True)
    return centred * lax.rsqrt(variance + EPSILON) * (1.0 + scale) + shift


def weights_of(query_rows, key_rows, mask):
    scores = (
        jnp.einsum("qhd,khd->hqk", query_rows, key_rows, preferred_element_type=jnp.float32) * SCALE
    )
    return jnp.where(mask[None, :, :], jnp.exp(scores), 0.0)


def over_blocks(count, step_fn, carry):
    block = math.gcd(count, 512)

    def advance(index, state):
        return step_fn(state, index * block, block)

    return lax.fori_loop(0, count // block, advance, carry)


def on_device(
    frames,
    skip_in,
    lengths,
    voiced,
    time_steps,
    time_table,
    skip_weight,
    skip_bias,
    adaptive_weight,
    adaptive_bias,
    merged_weight,
    output_weight,
    output_bias,
    up_weight,
    up_bias,
    down_weight,
    down_bias,
    cotangent,
):
    rows = frames.shape[1]
    width = frames.shape[2]
    lengths_here = lengths[0]
    voiced_here = voiced[0]
    device = lax.axis_index("blk")
    position = device * rows + jnp.arange(rows, dtype=jnp.int32)
    segment, offset, valid, member = frame_facts(lengths_here, voiced_here, position)
    cosine, sine = turn_tables(offset, HD)

    def key_mask(first_frame, count):
        key_position = first_frame + jnp.arange(count, dtype=jnp.int32)
        key_segment, key_offset, key_valid, key_member = frame_facts(
            lengths_here, voiced_here, key_position
        )
        return (segment[:, None] == key_segment[None, :]) & key_valid[None, :]

    def query_mask(first_frame, count):
        query_position = first_frame + jnp.arange(count, dtype=jnp.int32)
        query_segment, query_offset, query_valid, query_member = frame_facts(
            lengths_here, voiced_here, query_position
        )
        return (query_segment[:, None] == segment[None, :]) & valid[None, :]

    step_hot = (
        time_steps[0][:, None] == jnp.arange(time_table.shape[0], dtype=jnp.int32)[None, :]
    ).astype(jnp.float32)
    embed = jnp.dot(step_hot, time_table.astype(jnp.float32), precision=HIGHEST)
    cond, silu_back = jax.vjp(jax.nn.silu, embed)
    cond_low = cond.astype(jnp.bfloat16)
    per_utterance = jnp.dot(
        cond_low, adaptive_weight, preferred_element_type=jnp.float32
    ) + adaptive_bias.astype(jnp.float32)
    modulate = jnp.dot(member, per_utterance, precision=HIGHEST)
    joined = jnp.concatenate([frames[0], skip_in[0]], axis=1)
    first = jnp.dot(joined, skip_weight, preferred_element_type=jnp.float32) + skip_bias.astype(
        jnp.float32
    )
    normed, norm_back = jax.vjp(
        adaptive_norm, first, modulate[:, :width], modulate[:, width : 2 * width]
    )
    normed_low = normed.astype(jnp.bfloat16)
    merged = jnp.dot(normed_low, merged_weight, preferred_element_type=jnp.float32)
    query3 = rotate(merged[:, :width].reshape(rows, HEADS, HD), cosine, sine).astype(jnp.bfloat16)
    key3 = rotate(merged[:, width : 2 * width].reshape(rows, HEADS, HD), cosine, sine).astype(
        jnp.bfloat16
    )
    value3 = merged[:, 2 * width :].reshape(rows, HEADS, HD).astype(jnp.bfloat16)
    queries = query3.reshape(rows, width)
    keys = key3.reshape(rows, width)
    values = value3.reshape(rows, width)
    empty_rows = jnp.zeros((rows, width), jnp.float32)
    empty_heads = jnp.zeros((HEADS, rows), jnp.float32)
    piece_keys = lax.all_gather(keys, "blk", axis=0, tiled=True)
    piece_values = lax.all_gather(values, "blk", axis=0, tiled=True)

    def forward_add_block(state, inner, block):
        numer, total = state
        key_rows = lax.dynamic_slice_in_dim(piece_keys, inner, block, 0).reshape(block, HEADS, HD)
        value_rows = lax.dynamic_slice_in_dim(piece_values, inner, block, 0).reshape(
            block, HEADS, HD
        )
        expo = weights_of(query3, key_rows, key_mask(inner, block))
        total = total + jnp.sum(expo, axis=2)
        numer = numer + jnp.einsum(
            "hqk,khd->qhd",
            expo.astype(jnp.bfloat16),
            value_rows,
            preferred_element_type=jnp.float32,
        ).reshape(rows, width)
        return (numer, total)

    numer, total = over_blocks(piece_keys.shape[0], forward_add_block, (empty_rows, empty_heads))
    mixed3 = numer.reshape(rows, HEADS, HD) / jnp.transpose(total)[:, :, None]
    mixed_low = mixed3.reshape(rows, width).astype(jnp.bfloat16)
    attended = jnp.dot(
        mixed_low, output_weight, preferred_element_type=jnp.float32
    ) + output_bias.astype(jnp.float32)
    second = first + attended
    normed_two, norm_two_back = jax.vjp(
        adaptive_norm, second, modulate[:, 2 * width : 3 * width], modulate[:, 3 * width :]
    )
    normed_two_low = normed_two.astype(jnp.bfloat16)
    hidden = jnp.dot(
        normed_two_low, up_weight, preferred_element_type=jnp.float32
    ) + up_bias.astype(jnp.float32)
    activated, gelu_back = jax.vjp(jax.nn.gelu, hidden)
    activated_low = activated.astype(jnp.bfloat16)
    result = (
        second
        + jnp.dot(activated_low, down_weight, preferred_element_type=jnp.float32)
        + down_bias.astype(jnp.float32)
    )
    layer_out = result.astype(jnp.bfloat16)
    outer_grad = cotangent[0]
    outer_float = outer_grad.astype(jnp.float32)
    down_weight_term = jnp.einsum(
        "rf,rd->fd", activated_low, outer_grad, preferred_element_type=jnp.float32
    )
    down_bias_term = jnp.sum(outer_float, axis=0)
    grad_act = jnp.einsum("rd,fd->rf", outer_grad, down_weight, preferred_element_type=jnp.float32)
    (grad_hidden,) = gelu_back(grad_act)
    grad_hidden_low = grad_hidden.astype(jnp.bfloat16)
    up_weight_term = jnp.einsum(
        "rd,rf->df", normed_two_low, grad_hidden_low, preferred_element_type=jnp.float32
    )
    up_bias_term = jnp.sum(grad_hidden_low.astype(jnp.float32), axis=0)
    grad_normed_two = jnp.einsum(
        "rf,df->rd", grad_hidden_low, up_weight, preferred_element_type=jnp.float32
    )
    grad_second_norm, grad_scale_two, grad_shift_two = norm_two_back(grad_normed_two)
    grad_second = outer_float + grad_second_norm
    grad_attended = grad_second.astype(jnp.bfloat16)
    output_weight_term = jnp.einsum(
        "rd,re->de", mixed_low, grad_attended, preferred_element_type=jnp.float32
    )
    output_bias_term = jnp.sum(grad_attended.astype(jnp.float32), axis=0)
    grad_mixed3 = jnp.einsum(
        "re,de->rd", grad_attended, output_weight, preferred_element_type=jnp.float32
    ).reshape(rows, HEADS, HD)
    pull3 = (grad_mixed3 / jnp.transpose(total)[:, :, None]).astype(jnp.bfloat16)
    pulls = pull3.reshape(rows, width)
    correction = -jnp.transpose(jnp.sum(grad_mixed3 * mixed3, axis=2)) / total
    query_piece_keys = lax.all_gather(keys, "blk", axis=0, tiled=True)
    query_piece_values = lax.all_gather(values, "blk", axis=0, tiled=True)

    def query_add_block(state, inner, block):
        key_rows = lax.dynamic_slice_in_dim(query_piece_keys, inner, block, 0).reshape(
            block, HEADS, HD
        )
        value_rows = lax.dynamic_slice_in_dim(query_piece_values, inner, block, 0).reshape(
            block, HEADS, HD
        )
        expo = weights_of(query3, key_rows, key_mask(inner, block))
        pushed = jnp.einsum("qhd,khd->hqk", pull3, value_rows, preferred_element_type=jnp.float32)
        slope = (expo * (pushed + correction[:, :, None]) * SCALE).astype(jnp.bfloat16)
        return state + jnp.einsum(
            "hqk,khd->qhd", slope, key_rows, preferred_element_type=jnp.float32
        ).reshape(rows, width)

    grad_query = over_blocks(query_piece_keys.shape[0], query_add_block, empty_rows)
    corrections_all = lax.all_gather(correction, "blk", axis=1, tiled=True)
    piece_queries = lax.all_gather(queries, "blk", axis=0, tiled=True)
    piece_pulls = lax.all_gather(pulls, "blk", axis=0, tiled=True)

    def key_add_block(state, inner, block):
        grad_keys, grad_values = state
        query_rows = lax.dynamic_slice_in_dim(piece_queries, inner, block, 0).reshape(
            block, HEADS, HD
        )
        pull_rows = lax.dynamic_slice_in_dim(piece_pulls, inner, block, 0).reshape(block, HEADS, HD)
        expo = weights_of(query_rows, key3, query_mask(inner, block))
        pushed = jnp.einsum("qhd,khd->hqk", pull_rows, value3, preferred_element_type=jnp.float32)
        row_terms = lax.dynamic_slice_in_dim(corrections_all, inner, block, 1)
        slope = (expo * (pushed + row_terms[:, :, None]) * SCALE).astype(jnp.bfloat16)
        grad_keys = grad_keys + jnp.einsum(
            "hqk,qhd->khd", slope, query_rows, preferred_element_type=jnp.float32
        ).reshape(rows, width)
        grad_values = grad_values + jnp.einsum(
            "hqk,qhd->khd", expo.astype(jnp.bfloat16), pull_rows, preferred_element_type=jnp.float32
        ).reshape(rows, width)
        return (grad_keys, grad_values)

    grad_keys, grad_values = over_blocks(
        piece_queries.shape[0], key_add_block, (empty_rows, empty_rows)
    )
    query_back = rotate(grad_query.reshape(rows, HEADS, HD), cosine, -sine).reshape(rows, width)
    key_back = rotate(grad_keys.reshape(rows, HEADS, HD), cosine, -sine).reshape(rows, width)
    grad_merged = jnp.concatenate([query_back, key_back, grad_values], axis=1).astype(jnp.bfloat16)
    merged_weight_term = jnp.einsum(
        "rd,re->de", normed_low, grad_merged, preferred_element_type=jnp.float32
    )
    grad_normed = jnp.einsum(
        "re,de->rd", grad_merged, merged_weight, preferred_element_type=jnp.float32
    )
    grad_first_norm, grad_scale_one, grad_shift_one = norm_back(grad_normed)
    grad_first = (grad_second + grad_first_norm).astype(jnp.bfloat16)
    skip_weight_term = jnp.einsum(
        "rc,rd->cd", joined, grad_first, preferred_element_type=jnp.float32
    )
    skip_bias_term = jnp.sum(grad_first.astype(jnp.float32), axis=0)
    grad_joined = jnp.einsum(
        "rd,cd->rc", grad_first, skip_weight, preferred_element_type=jnp.float32
    )
    frames_grad = grad_joined[:, :width].astype(jnp.bfloat16)
    skip_grad = grad_joined[:, width:].astype(jnp.bfloat16)
    frame_modulate = jnp.concatenate(
        [grad_scale_one, grad_shift_one, grad_scale_two, grad_shift_two], axis=1
    )
    grad_modulate = jnp.dot(jnp.transpose(member), frame_modulate, precision=HIGHEST)
    adaptive_weight_term = jnp.dot(
        jnp.transpose(cond_low.astype(jnp.float32)), grad_modulate, precision=HIGHEST
    )
    adaptive_bias_term = jnp.sum(grad_modulate, axis=0)
    grad_cond = jnp.dot(
        grad_modulate,
        jnp.transpose(adaptive_weight),
        precision=HIGHEST,
        preferred_element_type=jnp.float32,
    )
    (grad_embed,) = silu_back(grad_cond)
    table_term = jnp.dot(jnp.transpose(grad_embed), step_hot, precision=HIGHEST)
    shares = (
        lax.psum_scatter(skip_weight_term, "blk", scatter_dimension=0, tiled=True),
        lax.psum_scatter(skip_bias_term, "blk", scatter_dimension=0, tiled=True),
        lax.psum_scatter(adaptive_weight_term, "blk", scatter_dimension=0, tiled=True),
        lax.psum_scatter(adaptive_bias_term, "blk", scatter_dimension=0, tiled=True),
        lax.psum_scatter(merged_weight_term, "blk", scatter_dimension=0, tiled=True),
        lax.psum_scatter(output_weight_term, "blk", scatter_dimension=0, tiled=True),
        lax.psum_scatter(output_bias_term, "blk", scatter_dimension=0, tiled=True),
        lax.psum_scatter(up_weight_term, "blk", scatter_dimension=0, tiled=True),
        lax.psum_scatter(up_bias_term, "blk", scatter_dimension=0, tiled=True),
        lax.psum_scatter(down_weight_term, "blk", scatter_dimension=0, tiled=True),
        lax.psum_scatter(down_bias_term, "blk", scatter_dimension=0, tiled=True),
        lax.psum_scatter(table_term, "blk", scatter_dimension=0, tiled=True),
    )
    summed = (
        lax.psum(shares[0].astype(jnp.bfloat16), "group").astype(jnp.float32),
        lax.psum(shares[1].astype(jnp.bfloat16), "group").astype(jnp.float32),
        lax.psum(shares[2].astype(jnp.bfloat16), "group").astype(jnp.float32),
        lax.psum(shares[3].astype(jnp.bfloat16), "group").astype(jnp.float32),
        lax.psum(shares[4].astype(jnp.bfloat16), "group").astype(jnp.float32),
        lax.psum(shares[5].astype(jnp.bfloat16), "group").astype(jnp.float32),
        lax.psum(shares[6].astype(jnp.bfloat16), "group").astype(jnp.float32),
        lax.psum(shares[7].astype(jnp.bfloat16), "group").astype(jnp.float32),
        lax.psum(shares[8].astype(jnp.bfloat16), "group").astype(jnp.float32),
        lax.psum(shares[9].astype(jnp.bfloat16), "group").astype(jnp.float32),
        lax.psum(shares[10].astype(jnp.bfloat16), "group").astype(jnp.float32),
        lax.psum(shares[11].astype(jnp.bfloat16), "group").astype(jnp.float32),
    )
    return (
        layer_out[None],
        frames_grad[None],
        skip_grad[None],
        jnp.transpose(summed[11]),
        summed[0],
        summed[1],
        summed[2],
        summed[3],
        summed[4],
        summed[5],
        summed[6],
        summed[7],
        summed[8],
        summed[9],
        summed[10],
    )


def halves(array):
    low = lax.broadcasted_iota(jnp.int32, array.shape, 1) < HD
    zero = jnp.zeros_like(array)
    return jnp.concatenate([jnp.where(low, array, zero), jnp.where(low, zero, array)], axis=0)


def pick_halves(stacked):
    rows = stacked.shape[0] // 2
    low = lax.broadcasted_iota(jnp.int32, (rows, stacked.shape[1]), 1) < HD
    return jnp.where(low, stacked[:rows], stacked[rows:])


def nt_dot(left, right):
    return lax.dot_general(
        left, right, (((1,), (1,)), ((), ())), preferred_element_type=jnp.float32
    )


def tn_dot(left, right):
    return lax.dot_general(
        left, right, (((0,), (0,)), ((), ())), preferred_element_type=jnp.float32
    )


def enter(partners):
    barrier = pltpu.get_barrier_semaphore()
    for partner in partners:
        pl.semaphore_signal(barrier, inc=1, device_id=partner, device_id_type=MESH_ID)
    pl.semaphore_wait(barrier, len(partners))


def remote(source, target, send_sem, recv_sem, partner):
    return pltpu.make_async_remote_copy(
        src_ref=source,
        dst_ref=target,
        send_sem=send_sem,
        recv_sem=recv_sem,
        device_id=partner,
        device_id_type=MESH_ID,
    )


def attend_forward_kernel(
    n,
    q_ref,
    k_ref,
    v_ref,
    segq_ref,
    segk_ref,
    mixed_ref,
    rq_ref,
    rk_ref,
    rv_ref,
    mh_ref,
    rt_ref,
    out_ref,
    send_sem,
    recv_sem,
    back_send,
    back_recv,
):
    b, g = lax.axis_index("blk"), lax.axis_index("group")
    rows = q_ref.shape[0]
    enter([((b + d) % n, g) for d in range(1, n)])

    def columns(block):
        return pl.ds(pl.multiple_of(block * LANES, LANES), LANES)

    def band(block):
        return pl.ds(pl.multiple_of(block * rows, rows), rows)

    sent = []
    for which, (source, target) in enumerate(((k_ref, rk_ref), (v_ref, rv_ref), (q_ref, rq_ref))):
        for d in range(1, n):
            p = (b + d) % n
            copy = remote(
                source.at[:, columns(p)],
                target.at[band(b)],
                send_sem.at[which, p],
                recv_sem.at[which, b],
                (p, g),
            )
            copy.start()
            sent.append(copy)
    for source, target in ((k_ref, rk_ref), (v_ref, rv_ref), (q_ref, rq_ref)):
        target[band(b), :] = source[:, columns(b)]

    def wait_in(which, source, target, d):
        p = (b + n - d) % n
        remote(
            source.at[:, columns(p)],
            target.at[band(p)],
            send_sem.at[which, p],
            recv_sem.at[which, p],
            (p, g),
        ).wait_recv()

    for d in range(1, n):
        wait_in(0, k_ref, rk_ref, d)
        wait_in(1, v_ref, rv_ref, d)

    def block_step(d, carry):
        p = (b + n - d) % n

        @pl.when(d > 0)
        def _():
            wait_in(2, q_ref, rq_ref, d)

        query = halves(rq_ref[band(p), :] * jnp.asarray(0.125, jnp.bfloat16))
        allow = segq_ref[band(p), :] == segk_ref[...]
        allow = jnp.concatenate([allow, allow], axis=0)
        expo = jnp.where(allow, jnp.exp(nt_dot(query, rk_ref[...])), 0.0)
        total = jnp.sum(expo, axis=1, keepdims=True)
        numer = jnp.dot(
            expo.astype(jnp.bfloat16), rv_ref[...], preferred_element_type=jnp.float32
        )
        inverse = 1.0 / total
        mixed = pick_halves(numer * inverse)
        mh_ref[band(p), :] = mixed
        rt_ref[band(p), :] = pick_halves(jnp.broadcast_to(inverse, numer.shape))
        out_ref[band(p), :] = mixed.astype(jnp.bfloat16)

        @pl.when(d > 0)
        def _():
            remote(
                out_ref.at[band(p)],
                mixed_ref.at[:, columns(b)],
                back_send.at[p],
                back_recv.at[b],
                (p, g),
            ).start()

        return carry

    def ordered(i, carry):
        return block_step((i + 1) % n, carry)

    lax.fori_loop(0, n, ordered, 0)
    mixed_ref[:, columns(b)] = out_ref[band(b), :]
    for copy in sent:
        copy.wait_send()
    for d in range(1, n):
        p = (b + d) % n
        copy = remote(
            out_ref.at[band(p)],
            mixed_ref.at[:, columns(p)],
            back_send.at[p],
            back_recv.at[p],
            (p, g),
        )
        copy.wait_send()
        copy.wait_recv()


def attend_forward(queries, keys, values, seg_q, seg_k, n):
    rows, width = queries.shape
    seq = rows * n
    low, full = jnp.bfloat16, jnp.float32
    shapes = [((rows, width), low)] + [((seq, LANES), low)] * 3 + [((seq, LANES), full)] * 2
    return pl.pallas_call(
        functools.partial(attend_forward_kernel, n),
        out_shape=[jax.ShapeDtypeStruct(*shape) for shape in shapes],
        in_specs=[VMEM_SPEC] * 5,
        out_specs=[VMEM_SPEC] * 6,
        scratch_shapes=[
            pltpu.VMEM((seq, LANES), low),
            pltpu.SemaphoreType.DMA((3, n)),
            pltpu.SemaphoreType.DMA((3, n)),
            pltpu.SemaphoreType.DMA((n,)),
            pltpu.SemaphoreType.DMA((n,)),
        ],
        compiler_params=pltpu.CompilerParams(
            collective_id=0, has_side_effects=True, vmem_limit_bytes=VMEM_LIMIT
        ),
        name="attend_forward",
    )(queries, keys, values, seg_q, seg_k)


def turn_back(array, cosine, sine):
    lane = lax.broadcasted_iota(jnp.int32, array.shape, 1) % HD
    other = jnp.where(
        lane < HD // 2,
        pltpu.roll(array, LANES - HD // 2, 1),
        pltpu.roll(array, HD // 2, 1),
    )
    return array * cosine + other * sine


def attend_backward_kernel(
    n,
    gm_ref,
    rq_ref,
    rk_ref,
    rv_ref,
    mh_ref,
    rt_ref,
    segq_ref,
    segk_ref,
    cos_ref,
    sin_ref,
    merged_ref,
    rg_ref,
    gq_ref,
    gk_ref,
    gv_ref,
    gk_acc,
    gv_acc,
    send_sem,
    recv_sem,
    back_send,
    back_recv,
):
    b, g = lax.axis_index("blk"), lax.axis_index("group")
    rows, width = gm_ref.shape
    enter([((b + d) % n, g) for d in range(1, n)])

    def columns(block, part=0):
        return pl.ds(pl.multiple_of(part * width + block * LANES, LANES), LANES)

    def band(block):
        return pl.ds(pl.multiple_of(block * rows, rows), rows)

    def incoming(p):
        return remote(
            gm_ref.at[:, columns(p)], rg_ref.at[band(p)], send_sem.at[p], recv_sem.at[p], (p, g)
        )

    def outward(part, source, p):
        return remote(
            source.at[band(p)],
            merged_ref.at[:, columns(b, part)],
            back_send.at[part, p],
            back_recv.at[part, b],
            (p, g),
        )

    for d in range(1, n):
        p = (b + d) % n
        remote(
            gm_ref.at[:, columns(p)], rg_ref.at[band(b)], send_sem.at[p], recv_sem.at[b], (p, g)
        ).start()
    rg_ref[band(b), :] = gm_ref[:, columns(b)]
    gk_acc[...] = jnp.zeros_like(gk_acc)
    gv_acc[...] = jnp.zeros_like(gv_acc)

    def block_step(i, carry):
        d = i
        p = (b + n - d) % n

        @pl.when(d > 0)
        def _():
            incoming(p).wait_recv()

        query = halves(rq_ref[band(p), :] * jnp.asarray(0.125, jnp.bfloat16))
        allow = segq_ref[band(p), :] == segk_ref[...]
        allow = jnp.concatenate([allow, allow], axis=0)
        expo = jnp.where(allow, jnp.exp(nt_dot(query, rk_ref[...])), 0.0)
        pull = rg_ref[band(p), :].astype(jnp.float32) * rt_ref[band(p), :]
        product = pull * mh_ref[band(p), :]
        low = lax.broadcasted_iota(jnp.int32, product.shape, 1) < HD
        correction = -jnp.concatenate(
            [
                jnp.sum(jnp.where(low, product, 0.0), axis=1, keepdims=True),
                jnp.sum(jnp.where(low, 0.0, product), axis=1, keepdims=True),
            ],
            axis=0,
        )
        pulls = halves(pull.astype(jnp.bfloat16))
        slope = (expo * (nt_dot(pulls, rv_ref[...]) + correction)).astype(jnp.bfloat16)
        grad_query = pick_halves(
            jnp.dot(slope, rk_ref[...], preferred_element_type=jnp.float32)
        )
        gq_ref[band(p), :] = turn_back(
            grad_query * 0.125, cos_ref[band(p), :], sin_ref[band(p), :]
        ).astype(jnp.bfloat16)

        @pl.when(d > 0)
        def _():
            outward(0, gq_ref, p).start()

        gk_acc[...] += tn_dot(query, slope)
        gv_acc[...] += tn_dot(pulls, expo.astype(jnp.bfloat16))
        return carry

    lax.fori_loop(0, n, block_step, 0)
    gv_ref[...] = jnp.transpose(gv_acc[...]).astype(jnp.bfloat16)
    for d in range(1, n):
        outward(2, gv_ref, (b + d) % n).start()
    gk_ref[...] = turn_back(jnp.transpose(gk_acc[...]), cos_ref[...], sin_ref[...]).astype(
        jnp.bfloat16
    )
    for d in range(1, n):
        outward(1, gk_ref, (b + d) % n).start()
    for part, source in enumerate((gq_ref, gk_ref, gv_ref)):
        merged_ref[:, columns(b, part)] = source[band(b), :]
    for d in range(1, n):
        p = (b + d) % n
        incoming(p).wait_send()
        for part, source in enumerate((gq_ref, gk_ref, gv_ref)):
            copy = remote(
                source.at[band(p)],
                merged_ref.at[:, columns(p, part)],
                back_send.at[part, p],
                back_recv.at[part, p],
                (p, g),
            )
            copy.wait_send()
            copy.wait_recv()


def attend_backward(grad_mixed, held, seg_q, seg_k, cosine, sine, n):
    rows, width = grad_mixed.shape
    seq = rows * n
    low, full = jnp.bfloat16, jnp.float32
    return pl.pallas_call(
        functools.partial(attend_backward_kernel, n),
        out_shape=jax.ShapeDtypeStruct((rows, 3 * width), low),
        in_specs=[VMEM_SPEC] * 10,
        out_specs=VMEM_SPEC,
        scratch_shapes=[
            pltpu.VMEM((seq, LANES), low),
            pltpu.VMEM((seq, LANES), low),
            pltpu.VMEM((seq, LANES), low),
            pltpu.VMEM((seq, LANES), low),
            pltpu.VMEM((LANES, seq), full),
            pltpu.VMEM((LANES, seq), full),
            pltpu.SemaphoreType.DMA((n,)),
            pltpu.SemaphoreType.DMA((n,)),
            pltpu.SemaphoreType.DMA((3, n)),
            pltpu.SemaphoreType.DMA((3, n)),
        ],
        compiler_params=pltpu.CompilerParams(
            collective_id=1, has_side_effects=True, vmem_limit_bytes=VMEM_LIMIT
        ),
        name="attend_backward",
    )(grad_mixed, *held, seg_q, seg_k, cosine, sine)


def weight_grad_kernel(kinds, n, m, *refs):
    count = len(kinds)
    xs, gs = refs[:count], refs[count : 2 * count]
    small_ref, extra_ref = refs[2 * count : 2 * count + 2]
    at = 2 * count + 2
    outs = refs[at : at + count]
    small_out, extra_out = refs[at + count : at + count + 2]
    at += count + 2
    x_all, g_all, y_out, y_in, z_out, z_in, own = (
        refs[at + i * count : at + (i + 1) * count] for i in range(7)
    )
    at += 7 * count
    (
        s_in,
        s_sum,
        gather_send,
        gather_recv,
        y_send,
        y_recv,
        z_send,
        z_recv,
        last_send,
        last_recv,
        s_send,
        s_recv,
    ) = refs[at:]
    b, g = lax.axis_index("blk"), lax.axis_index("group")
    y, z = b % 2, b // 2
    depth = n // 2
    enter([(b, (g + d) % m) for d in range(1, m)] + [((b + d) % n, g) for d in range(1, n)])
    part = small_ref.shape[1] // n

    def chunk(index, size):
        return pl.ds(pl.multiple_of(index * size, size), size)

    gathers = {}
    for t in range(count):
        for side, (source, target) in enumerate(((xs[t], x_all[t]), (gs[t], g_all[t]))):
            split = kinds[t] == (side == 0)
            size = target.shape[2]
            for d in range(1, m):
                p = (g + d) % m
                copy = remote(
                    source.at[:, chunk(p, size)] if split else source,
                    target.at[g],
                    gather_send.at[t, side, d],
                    gather_recv.at[t, side, d],
                    (b, p),
                )
                copy.start()
                gathers[t, side, d] = copy
    smalls = []
    for d in range(1, n):
        p = (b + d) % n
        copy = remote(
            small_ref.at[:, chunk(p, part)], s_in.at[d], s_send.at[0, d], s_recv.at[0, d], (p, g)
        )
        copy.start()
        smalls.append(copy)
    for d in range(1, m):
        copy = remote(
            extra_ref, extra_out.at[g], s_send.at[1, d], s_recv.at[1, d], (b, (g + d) % m)
        )
        copy.start()
        smalls.append(copy)
    extra_out[g] = extra_ref[...]
    for t in range(count):
        for side, (source, target) in enumerate(((xs[t], x_all[t]), (gs[t], g_all[t]))):
            split = kinds[t] == (side == 0)
            size = target.shape[2]
            target[g] = source[:, chunk(g, size)] if split else source[...]

    y_copies, z_copies, last_copies = {}, {}, {}

    def products(t):
        for side in range(2):
            for d in range(1, m):
                gathers[t, side, d].wait_recv()
        x_ref, g_ref = x_all[t], g_all[t]
        deep = x_ref.shape[0] * x_ref.shape[1]
        size = own[t].shape[1]

        def product(block):
            left = x_ref[:, :, chunk(block, size)].reshape(deep, size)
            right = g_ref[...].reshape(deep, g_ref.shape[2])
            return tn_dot(left, right)

        for zi in (2, 1, 3, 0):
            zp = (z + zi) % depth
            y_out[t][zi] = product(zp * 2 + (1 - y)).astype(jnp.bfloat16)
            copy = remote(
                y_out[t].at[zi],
                y_in[t].at[zi],
                y_send.at[t, zi],
                y_recv.at[t, zi],
                (z * 2 + (1 - y), g),
            )
            copy.start()
            y_copies[t, zi] = copy
        for zi in (2, 1, 3, 0):
            zp = (z + zi) % depth
            own[t][zi] = product(zp * 2 + y)

    def over_z(t):
        for zi in (2, 1, 3):
            zp = (z + zi) % depth
            y_copies[t, zi].wait_recv()
            z_out[t][zi] = (own[t][zi] + y_in[t][zi].astype(jnp.float32)).astype(jnp.bfloat16)
            copy = remote(
                z_out[t].at[zi],
                z_in[t].at[zi],
                z_send.at[t, zi],
                z_recv.at[t, zi],
                (zp * 2 + y, g),
            )
            copy.start()
            z_copies[t, zi] = copy

    def finish(t):
        y_copies[t, 0].wait_recv()
        total = own[t][0] + y_in[t][0].astype(jnp.float32)
        for zi in (1, 3, 2):
            z_copies[t, zi].wait_recv()
            total = total + z_in[t][zi].astype(jnp.float32)
        outs[t][g] = total.astype(jnp.bfloat16)
        for d in range(1, m):
            copy = remote(
                outs[t].at[g],
                outs[t].at[g],
                last_send.at[t, d],
                last_recv.at[t, d],
                (b, (g + d) % m),
            )
            copy.start()
            last_copies[t, d] = copy

    for step in range(count + 2):
        if step < count:
            products(step)
        if step == 0:
            s_in[0] = small_ref[:, chunk(b, part)]
            for d in range(1, n):
                smalls[d - 1].wait_recv()
            s_sum[...] = jnp.sum(s_in[...], axis=0).astype(jnp.bfloat16)
            small_out[g, b] = s_sum[...]
            for d in range(1, n):
                copy = remote(
                    s_sum, small_out.at[g, b], s_send.at[2, d], s_recv.at[2, d], ((b + d) % n, g)
                )
                copy.start()
                smalls.append(copy)
        if step == 1:
            for d in range(1, n):
                smalls[n - 1 + m - 1 + d - 1].wait_recv()
            for d in range(1, m):
                copy = remote(
                    small_out.at[g],
                    small_out.at[g],
                    s_send.at[3, d],
                    s_recv.at[3, d],
                    (b, (g + d) % m),
                )
                copy.start()
                smalls.append(copy)
        if 0 <= step - 1 < count:
            over_z(step - 1)
        if 0 <= step - 2 < count:
            finish(step - 2)
    for copy in last_copies.values():
        copy.wait_recv()
    for copy in smalls[n - 1 : n - 1 + m - 1] + smalls[-(m - 1) :]:
        copy.wait_recv()
    for group in (gathers, y_copies, z_copies, last_copies):
        for copy in group.values():
            copy.wait_send()
    for copy in smalls:
        copy.wait_send()


def weight_grads(tasks, small, extra, n, m):
    low, full = jnp.bfloat16, jnp.float32
    xs, gs, kinds = zip(*tasks)
    depth = n // 2
    outs, x_all, g_all, y_out, own = [], [], [], [], []
    for left, right, split_left in tasks:
        rows, inner = left.shape
        outer = right.shape[1]
        inner, outer = (inner // m, outer) if split_left else (inner, outer // m)
        block = (inner // n, outer)
        outs.append(jax.ShapeDtypeStruct((m, *block), low))
        x_all.append(pltpu.VMEM((m, rows, inner), low))
        g_all.append(pltpu.VMEM((m, rows, outer), low))
        y_out.append(pltpu.VMEM((depth, *block), low))
        own.append(pltpu.VMEM((depth, *block), full))
    count = len(tasks)
    part = small.shape[1] // n
    outs.append(jax.ShapeDtypeStruct((m, n, small.shape[0], part), low))
    outs.append(jax.ShapeDtypeStruct((m, *extra.shape), low))
    sems = [pltpu.SemaphoreType.DMA((count, 2, m))] * 2
    sems += [pltpu.SemaphoreType.DMA((count, depth))] * 4
    sems += [pltpu.SemaphoreType.DMA((count, m))] * 2
    sems += [pltpu.SemaphoreType.DMA((4, max(n, m)))] * 2
    return pl.pallas_call(
        functools.partial(weight_grad_kernel, kinds, n, m),
        out_shape=outs,
        in_specs=[VMEM_SPEC] * (2 * count + 2),
        out_specs=[VMEM_SPEC] * (count + 2),
        scratch_shapes=x_all
        + g_all
        + y_out * 4
        + own
        + [
            pltpu.VMEM((n, small.shape[0], part), full),
            pltpu.VMEM((small.shape[0], part), low),
        ]
        + sems,
        compiler_params=pltpu.CompilerParams(
            collective_id=2, has_side_effects=True, vmem_limit_bytes=VMEM_LIMIT
        ),
        name="weight_grads",
    )(*xs, *gs, small, extra)


def by_heads(
    n,
    m,
    frames,
    skip_in,
    lengths,
    voiced,
    time_steps,
    time_table,
    skip_weight,
    skip_bias,
    adaptive_weight,
    adaptive_bias,
    merged_weight,
    output_weight,
    output_bias,
    up_weight,
    up_bias,
    down_weight,
    down_bias,
    cotangent,
):
    rows, width = frames.shape[1:]
    ff = up_weight.shape[1]
    low, full = jnp.bfloat16, jnp.float32
    b, g = lax.axis_index("blk"), lax.axis_index("group")
    everywhere = jnp.arange(rows * n, dtype=jnp.int32)
    segment, offset, valid, member_all = frame_facts(lengths[0], voiced[0], everywhere)
    cosine_all, sine_all = turn_tables(offset, HD)
    seg_q = segment.astype(full)[:, None]
    seg_k = jnp.where(valid, segment, -1).astype(full)[None, :]
    cos_lanes = jnp.tile(cosine_all, (1, LANES // cosine_all.shape[1]))
    sin_lanes = jnp.tile(
        jnp.concatenate([sine_all, -sine_all], axis=1), (1, LANES // (2 * sine_all.shape[1]))
    )
    cosine = lax.dynamic_slice_in_dim(cosine_all, b * rows, rows, 0)
    sine = lax.dynamic_slice_in_dim(sine_all, b * rows, rows, 0)
    member = lax.dynamic_slice_in_dim(member_all, b * rows, rows, 0)

    step_hot = (
        time_steps[0][:, None] == jnp.arange(time_table.shape[0], dtype=jnp.int32)[None, :]
    ).astype(full)
    embed = jnp.dot(step_hot, time_table.astype(full), precision=HIGHEST)
    cond_low = jax.nn.silu(embed).astype(low)
    per_utterance = jnp.dot(
        cond_low, adaptive_weight, preferred_element_type=full
    ) + adaptive_bias.astype(full)
    modulate = jnp.dot(member, per_utterance, precision=HIGHEST)
    joined = jnp.concatenate([frames[0], skip_in[0]], axis=1)
    first = jnp.dot(joined, skip_weight, preferred_element_type=full) + skip_bias.astype(full)
    normed, norm_back = jax.vjp(
        adaptive_norm, first, modulate[:, :width], modulate[:, width : 2 * width]
    )
    normed_low = normed.astype(low)
    merged = jnp.dot(normed_low, merged_weight, preferred_element_type=full)

    def turned(part):
        heads = part.reshape(rows, HEADS, HD)
        return rotate(heads, cosine, sine).astype(low).reshape(rows, width)

    queries = turned(merged[:, :width])
    keys = turned(merged[:, width : 2 * width])
    values = merged[:, 2 * width :].astype(low)
    mixed_low, *held = attend_forward(queries, keys, values, seg_q, seg_k, n)

    attended = jnp.dot(mixed_low, output_weight, preferred_element_type=full) + output_bias.astype(
        full
    )
    second = first + attended
    normed_two, norm_two_back = jax.vjp(
        adaptive_norm, second, modulate[:, 2 * width : 3 * width], modulate[:, 3 * width :]
    )
    normed_two_low = normed_two.astype(low)
    hidden = jnp.dot(normed_two_low, up_weight, preferred_element_type=full) + up_bias.astype(full)
    activated, gelu_back = jax.vjp(jax.nn.gelu, hidden)
    activated_low = activated.astype(low)
    result = (
        second
        + jnp.dot(activated_low, down_weight, preferred_element_type=full)
        + down_bias.astype(full)
    )
    layer_out = result.astype(low)
    outer_grad = cotangent[0]
    outer_float = outer_grad.astype(full)
    grad_act = jnp.einsum("rd,fd->rf", outer_grad, down_weight, preferred_element_type=full)
    (grad_hidden,) = gelu_back(grad_act)
    grad_hidden_low = grad_hidden.astype(low)
    grad_normed_two = jnp.einsum(
        "rf,df->rd", grad_hidden_low, up_weight, preferred_element_type=full
    )
    grad_second_norm, grad_scale_two, grad_shift_two = norm_two_back(grad_normed_two)
    grad_second = outer_float + grad_second_norm
    grad_attended = grad_second.astype(low)
    grad_mixed = jnp.einsum(
        "re,de->rd", grad_attended, output_weight, preferred_element_type=full
    ).astype(low)
    grad_merged = attend_backward(grad_mixed, held, seg_q, seg_k, cos_lanes, sin_lanes, n)
    grad_normed = jnp.einsum("re,de->rd", grad_merged, merged_weight, preferred_element_type=full)
    grad_first_norm, grad_scale_one, grad_shift_one = norm_back(grad_normed)
    grad_first = (grad_second + grad_first_norm).astype(low)
    grad_joined = jnp.einsum("rd,cd->rc", grad_first, skip_weight, preferred_element_type=full)
    frames_grad = grad_joined[:, :width].astype(low)
    skip_grad = grad_joined[:, width:].astype(low)

    frame_modulate = jnp.concatenate(
        [grad_scale_one, grad_shift_one, grad_scale_two, grad_shift_two], axis=1
    )
    grad_modulate = jnp.dot(jnp.transpose(member), frame_modulate, precision=HIGHEST)
    utterances = grad_modulate.shape[0]
    biases = jnp.concatenate(
        [
            jnp.sum(grad_hidden_low.astype(full), axis=0),
            jnp.sum(grad_first.astype(full), axis=0),
            jnp.sum(grad_attended.astype(full), axis=0),
            jnp.sum(outer_float, axis=0),
            jnp.zeros((width,), full),
        ]
    ).reshape(2, 4 * width)
    small = jnp.concatenate([grad_modulate, biases, jnp.zeros((6, 4 * width), full)], axis=0)
    extra = jnp.concatenate([embed, step_hot, jnp.zeros((utterances, 96), full)], axis=1)
    extra = jnp.concatenate([extra, jnp.zeros_like(extra)], axis=0).astype(low)

    quarter = ff // (n * m)
    activated_turned = (
        activated_low.reshape(rows, n, m, quarter).transpose(0, 2, 1, 3).reshape(rows, ff)
    )
    *terms, small_all, extra_all = weight_grads(
        (
            (activated_turned, outer_grad, True),
            (normed_two_low, grad_hidden_low, False),
            (mixed_low, grad_attended, False),
            (normed_low, grad_merged, False),
            (joined, grad_first, False),
        ),
        small,
        extra,
        n,
        m,
    )
    down_grad = terms[0].astype(full).reshape(-1, width)
    up_grad, output_grad, merged_grad, skip_grad_weight = (
        jnp.transpose(term, (1, 0, 2)).reshape(term.shape[1], -1).astype(full) for term in terms[1:]
    )
    small_all = jnp.transpose(small_all, (0, 2, 1, 3)).reshape(m, small.shape[0], 4 * width)
    modulate_low = small_all[:, :utterances].reshape(m * utterances, 4 * width)
    bias_sums = jnp.sum(small_all[:, utterances : utterances + 2].astype(full), axis=0).reshape(-1)
    embed_all = extra_all[:, :utterances, :width].reshape(m * utterances, width).astype(full)
    hot_all = extra_all[:, :utterances, width : width + time_table.shape[0]].reshape(
        m * utterances, -1
    )
    share = width // n
    embed_here = lax.dynamic_slice_in_dim(embed_all, b * share, share, 1)
    cond_here, silu_back = jax.vjp(jax.nn.silu, embed_here)
    adaptive_weight_grad = jnp.einsum(
        "ur,uc->rc", cond_here.astype(low), modulate_low, preferred_element_type=full
    )
    adaptive_bias_sums = jnp.sum(modulate_low.astype(full), axis=0)
    weight_here = lax.dynamic_slice_in_dim(adaptive_weight, b * share, share, 0)
    grad_cond = jnp.einsum("uc,rc->ur", modulate_low, weight_here, preferred_element_type=full)
    (grad_embed,) = silu_back(grad_cond)
    table_grad = jnp.dot(jnp.transpose(hot_all.astype(full)), grad_embed, precision=HIGHEST)

    def own_part(vector):
        size = vector.shape[0] // n
        return lax.dynamic_slice_in_dim(vector, b * size, size, 0)

    return (
        layer_out[None],
        frames_grad[None],
        skip_grad[None],
        table_grad,
        skip_grad_weight,
        own_part(bias_sums[4 * width : 5 * width]),
        adaptive_weight_grad,
        own_part(adaptive_bias_sums),
        merged_grad,
        output_grad,
        own_part(bias_sums[5 * width : 6 * width]),
        up_grad,
        own_part(bias_sums[: 4 * width]),
        down_grad,
        own_part(bias_sums[6 * width : 7 * width]),
    )


def solution(mesh):
    in_specs = (
        P("group", "blk", None),
        P("group", "blk", None),
        P("group", None),
        P("group", None),
        P("group", None),
        P(),
        P(),
        P(),
        P(),
        P(),
        P(),
        P(),
        P(),
        P(),
        P(),
        P(),
        P(),
        P("group", "blk", None),
    )
    out_specs = (
        P("group", "blk", None),
        P("group", "blk", None),
        P("group", "blk", None),
        P(None, "blk"),
        P("blk", None),
        P("blk"),
        P("blk", None),
        P("blk"),
        P("blk", None),
        P("blk", None),
        P("blk"),
        P("blk", None),
        P("blk"),
        P("blk", None),
        P("blk"),
    )
    n, m = mesh.shape["blk"], mesh.shape["group"]
    fits = n % 2 == 0 and n // 2 == 4 and n * LANES == HEADS * HD and m == 4
    body = functools.partial(by_heads, n, m) if fits else on_device
    return jax.shard_map(
        body, mesh=mesh, in_specs=in_specs, out_specs=out_specs, check_vma=False
    )
```
